32 devices in a mesh: grp: 2 (over core), blk: 16 (over z, y, x).
Axes of the slice: x: 2, y: 2, z: 4, core: 2. Of those that a mesh axis runs over, the one named last changes fastest.
Arguments:
- queries: bfloat16 [8192, 2048], P(('grp', 'blk')), may hold values from -6 to 6
- keys: bfloat16 [8192, 2048], P(('grp', 'blk')), may hold values from -6 to 6
- values: bfloat16 [8192, 2048], P(('grp', 'blk')), may hold values from -6 to 6
- memory_keys: bfloat16 [256, 64, 2048], P(('grp', 'blk')), may hold values from -6 to 6
- memory_values: bfloat16 [256, 64, 2048], P(('grp', 'blk')), may hold values from -6 to 6
- owners: int32 [64, 16, 8], P(('grp', 'blk')), may hold values from 0 to 31, all different within a row; in each aligned block of 32 rows (0 to 31, 32 to 63, ..., all dimensions but the last counted through in order) at most 10 rows name the same one
- slots: int32 [64, 16, 8], P(('grp', 'blk')), may hold values from 0 to 7
- gate_logit: float32 [16], replicated, may hold values from -2 to 2
Outputs:
- mixed: bfloat16 [8192, 2048], P(('grp', 'blk'))
The draws below stay inside these ranges and needn't reach their ends.
Inputs may be any that keep to these rules, and one draw needn't show every extreme that they name: Each pair of a query block and a head names 8 different owners; the rows of one device name any one owner 10 times at most, and on some devices some owner exactly 10 times.
All inputs are finite; a program needn't handle non-finite values.
Results may differ from the reference program's by a relative error of at most 0.005.
Values may be sent and summed in bfloat16 or wider, within the bound.
A program may use at most 128 MiB of HBM per device.

```python
import math
import jax
import jax.numpy as jnp
import numpy as np
from jax import lax

H = 16
DH = 128
D = 2048
QBLK = 128
MB = 64
RET = 8
MBLK_DEV = 8
QB_DEV = 2
TOKENS = 8192
LENGTH = 4096
QBLOCKS = 64
MBLOCKS = 256
BAND = 768
CAP = 10
N_GRP = 2
DEVICES = 32


def hot_field(key, row_count, col_count):
    key_base = jax.random.fold_in(key, 0)
    field = jax.random.truncated_normal(key_base, -5.0, 5.0, (row_count, col_count), jnp.float32)
    return field


def draw_queries(key, part):
    return hot_field(jax.random.fold_in(key, 11), TOKENS, D).astype(jnp.bfloat16)


def draw_keys(key, part):
    return hot_field(jax.random.fold_in(key, 23), TOKENS, D).astype(jnp.bfloat16)


def draw_memory_keys(key, part):
    field = hot_field(jax.random.fold_in(key, 37), MBLOCKS * MB, D)
    return field.reshape(MBLOCKS, MB, D).astype(jnp.bfloat16)


def plant(array, stream_key, low, top_value):
    longest = array.shape.index(max(array.shape))
    spots = []
    for shift in (0, 1):
        where = [jax.random.randint(jax.random.fold_in(stream_key, axis), (), 0, length) for axis, length in enumerate(array.shape)]
        where[longest] = (where[longest] + shift) % array.shape[longest]
        spots.append(tuple(where))
    return array.at[spots[0]].set(low).at[spots[1]].set(top_value)


def block_levels(rng, extent, cuts, least, high):
    def one(position, blocks):
        heights = jax.random.uniform(jax.random.fold_in(jax.random.fold_in(rng, 6), position), (blocks,), jnp.float32, least / len(cuts), high / len(cuts))
        return jnp.repeat(jnp.exp(heights), extent[position] // blocks).reshape((-1,) + (1,) * (len(extent) - position - 1))

    loudness = one(*cuts[0])
    for cut in cuts[1:]:
        loudness = loudness * one(*cut)
    return loudness


def rank_table(number_of, lean):
    portions = [(1 << 20) // math.isqrt(grade ** lean) + 1 for grade in range(1, number_of + 1)]
    spread = 1 + sum(portions) // (1 << 30)
    return np.cumsum(np.array([max(1, weight // spread) for weight in portions]))


def ranked(rng, dims, amount, slope):
    table = rank_table(amount, slope)
    ticket = jax.random.randint(jax.random.fold_in(rng, 1), dims, 0, int(table[amount - 1]))
    standing = jnp.searchsorted(jnp.asarray(table, jnp.int32), ticket, side="right")
    return jax.random.permutation(jax.random.fold_in(rng, 2), amount)[standing].astype(jnp.int32)


def assign_block(rng, own, number, rows, amount, top, reach, lean):
    ranking = jax.random.permutation(rng, amount)
    heavy_load, usual = load_shares(amount, rows * top, reach, lean, True), load_shares(amount, rows * top, reach, lean, False)
    places = jnp.arange(amount)

    def named(sizes, turn):
        used = int((sizes > 0).sum())
        fixed = max(1, used // 4)
        shifted = fixed + (places - fixed + turn * (used - fixed)) % max(1, amount - fixed)
        return jnp.zeros((amount,), jnp.int32).at[ranking[jnp.where(places < fixed, places, shifted)]].set(jnp.asarray(sizes, jnp.int32))

    sizes = jnp.where(number % 4 == 0, named(heavy_load, number // 4), named(usual, number - number // 4 - 1))
    mixed = jax.random.permutation(jax.random.fold_in(own, 3), amount)
    source_of, receiver = mixed[0:amount // 2 * 2:2], mixed[1:amount // 2 * 2:2]
    room = jnp.minimum(sizes[source_of] - 1, reach - sizes[receiver]) // 2
    room = jnp.where((source_of == ranking[0]) | (receiver == ranking[0]) | (sizes[receiver] == 0), 0, jnp.maximum(room, 0))
    shifted = jax.random.randint(jax.random.fold_in(own, 4), (amount // 2,), 0, 1 << 20) % (room + 1)
    sizes = sizes.at[source_of].add(-shifted).at[receiver].add(shifted)
    members = jnp.searchsorted(jnp.cumsum(sizes), jnp.arange(rows * top), side="right").astype(jnp.int32)
    grid = members.reshape(top, rows).T
    grid = grid[jax.random.permutation(jax.random.fold_in(own, 1), rows)]
    turn = jax.random.randint(jax.random.fold_in(own, 2), (rows, 1), 0, top)
    return jnp.take_along_axis(grid, (jnp.arange(top)[None, :] + turn) % top, axis=1)


def load_shares(amount, total, reach, slope, full):
    weights = [(1 << 20) // math.isqrt(rank ** slope) + 1 for rank in range(1, amount + 1)]
    largest = reach if full else min(reach, max(-(-total // amount), total * weights[0] // sum(weights)))
    least = 1 if total - largest >= amount - 1 else 0
    counts, surplus = [largest] + [least] * (amount - 1), total - largest - least * (amount - 1)
    while surplus > 0:
        free = [i for i in range(1, amount) if counts[i] < largest] or [i for i in range(1, amount) if counts[i] < reach]
        mass, remaining = sum([weights[i] for i in free]), surplus
        for i in free:
            extra = min(reach - counts[i], max(1, remaining * weights[i] // mass), surplus)
            counts[i] = counts[i] + extra
            surplus = surplus - extra
    return np.array(counts)


def gaussian(own_key, dims, width, most, shards=(), held_as=jnp.bfloat16):
    values = width * jax.random.normal(own_key, dims, jnp.float32)
    if shards:
        values = values * block_levels(own_key, dims, shards, -0.22, 0.18)
    return jnp.clip(values, -most, most).astype(held_as)


def setup_inputs(seed: int = 0) -> dict:
    key_of = jax.random.split(jax.random.key(seed), 9)
    queries = draw_queries(jax.random.fold_in(key_of[8], 71), 0)
    keys = draw_keys(jax.random.fold_in(key_of[8], 71), 0)
    values = gaussian(key_of[2], (TOKENS, D), 1.0, 6.0, ((0, 32),))
    memory_keys = draw_memory_keys(jax.random.fold_in(key_of[8], 71), 0)
    memory_values = gaussian(key_of[4], (MBLOCKS, MB, D), 1.0, 6.0, ((0, 32),))
    owners_keys = jax.random.split(jax.random.fold_in(key_of[5], 1), QBLOCKS * H // (QB_DEV * H))
    owners_turns = jax.random.permutation(jax.random.fold_in(key_of[5], 3), QBLOCKS * H // (QB_DEV * H))
    owners = jax.vmap(lambda own, number: assign_block(jax.random.fold_in(key_of[5], 2), own, number, QB_DEV * H, DEVICES, RET, CAP, 2))(owners_keys, owners_turns).reshape((QBLOCKS, H, RET))
    slots = plant(ranked(key_of[6], (QBLOCKS, H, RET), MBLK_DEV, 2), jax.random.fold_in(key_of[6], 3), 0, MBLK_DEV - 1).astype(jnp.int32)
    gate_logit = jnp.clip(jax.random.uniform(key_of[7], (H,), jnp.float32, -2.0, 2.0), -2.0, 2.0)
    return dict(queries=queries, keys=keys, values=values, memory_keys=memory_keys, memory_values=memory_values, owners=owners, slots=slots, gate_logit=gate_logit)


masked_score = -1e+30

def band_sequence(query_seq, key_seq, value_seq):
    score_scale = 1.0 / math.sqrt(DH)
    keys_padded = jnp.concatenate([jnp.zeros((BAND, H, DH), key_seq.dtype), key_seq], axis=0)
    values_padded = jnp.concatenate([jnp.zeros((BAND, H, DH), value_seq.dtype), value_seq], axis=0)

    def attend_block(block_index):
        first_row = block_index * QBLK
        query_block = lax.dynamic_slice_in_dim(query_seq, first_row, QBLK, 0).astype(jnp.float32)
        key_block = lax.dynamic_slice_in_dim(keys_padded, first_row, BAND + QBLK, 0).astype(jnp.float32)
        value_block = lax.dynamic_slice_in_dim(values_padded, first_row, BAND + QBLK, 0).astype(jnp.float32)
        scores = jnp.einsum('qhd,khd->hqk', query_block, key_block) * score_scale
        query_pos = first_row + jnp.arange(QBLK, dtype=jnp.int32)
        key_pos = first_row - BAND + jnp.arange(BAND + QBLK, dtype=jnp.int32)
        offset = query_pos[:, None] - key_pos[None, :]
        allowed = (key_pos[None, :] >= 0) & (offset >= 0) & (offset <= BAND)
        scores = jnp.where(allowed[None], scores, masked_score)
        row_max = lax.optimization_barrier(jnp.max(scores, axis=2, keepdims=True))
        raised = jnp.exp(scores - row_max)
        weights = (raised / lax.optimization_barrier(jnp.sum(raised, axis=2, keepdims=True))).astype(jnp.bfloat16)
        return jnp.einsum('hqk,khd->qhd', weights.astype(jnp.float32), value_block)
    attended = lax.map(attend_block, jnp.arange(LENGTH // QBLK, dtype=jnp.int32))
    return attended.reshape(LENGTH, H, DH)

def reference(queries, keys, values, memory_keys, memory_values, owners, slots, gate_logit):
    score_scale = 1.0 / math.sqrt(DH)
    query_heads = queries.reshape(N_GRP, LENGTH, H, DH)
    key_seqs = keys.reshape(N_GRP, LENGTH, H, DH)
    value_seqs = values.reshape(N_GRP, LENGTH, H, DH)
    band_parts = []
    for sequence in range(N_GRP):
        band_parts.append(band_sequence(query_heads[sequence], key_seqs[sequence], value_seqs[sequence]))
    band_out = jnp.concatenate(band_parts, axis=0)
    key_heads = memory_keys.reshape(MBLOCKS, MB, H, DH)
    value_heads = memory_values.reshape(MBLOCKS, MB, H, DH)
    block_ids = owners * MBLK_DEV + slots
    head_ids = jnp.arange(H, dtype=jnp.int32)[:, None]
    flat_queries = queries.reshape(TOKENS, H, DH)

    def attend_memory(block_index):
        query_block = lax.dynamic_slice_in_dim(flat_queries, block_index * QBLK, QBLK, 0).astype(jnp.float32)
        chosen = block_ids[block_index]
        key_block = key_heads[chosen, :, head_ids, :].astype(jnp.float32)
        value_block = value_heads[chosen, :, head_ids, :].astype(jnp.float32)
        scores = jnp.einsum('qhd,hrkd->hqrk', query_block, key_block) * score_scale
        row_max = lax.optimization_barrier(jnp.max(scores, axis=(2, 3), keepdims=True))
        raised = jnp.exp(scores - row_max)
        weights = (raised / lax.optimization_barrier(jnp.sum(raised, axis=(2, 3), keepdims=True))).astype(jnp.bfloat16)
        return jnp.einsum('hqrk,hrkd->qhd', weights.astype(jnp.float32), value_block)
    memory_out = lax.map(attend_memory, jnp.arange(QBLOCKS, dtype=jnp.int32)).reshape(TOKENS, H, DH)
    gate_share = jax.nn.sigmoid(gate_logit.astype(jnp.float32))[None, :, None]
    mixed = gate_share * memory_out + (1.0 - gate_share) * band_out
    return mixed.reshape(TOKENS, D).astype(jnp.bfloat16)
```

```python
import functools
import math

import jax
import jax.numpy as jnp
from jax import lax
from jax.experimental import pallas as pl
from jax.experimental.pallas import tpu as pltpu
from jax.sharding import PartitionSpec as P

H = 16
QBLK = 128
MB = 64
RET = 8
DH = 128
BEHIND = 3
LOG2E = 1.4426950408889634
SCALE2 = LOG2E / math.sqrt(DH)
LOW = -1e30


def from_behind(value, axis, steps):
    count = lax.axis_size(axis)
    return lax.ppermute(value, axis, [(i, i + steps) for i in range(count - steps)])


def pick_kernel(req_ref, key_ref, value_ref, out_ref, sem, *, count):
    def step(i, carry):
        code = jnp.maximum(req_ref[i], 0)
        block = code // H
        col = pl.multiple_of((code % H) * DH, DH)
        pltpu.make_async_copy(key_ref.at[block, :, pl.ds(col, DH)], out_ref.at[i, 0], sem).start()
        pltpu.make_async_copy(value_ref.at[block, :, pl.ds(col, DH)], out_ref.at[i, 1], sem).start()
        return carry

    lax.fori_loop(0, count, step, 0)
    pltpu.make_async_copy(out_ref, out_ref, sem).wait()


def pick(requests, key_mem, value_mem):
    count = requests.shape[0]
    return pl.pallas_call(
        functools.partial(pick_kernel, count=count),
        out_shape=jax.ShapeDtypeStruct((count, 2, MB, DH), key_mem.dtype),
        in_specs=[
            pl.BlockSpec(memory_space=pltpu.SMEM),
            pl.BlockSpec(memory_space=pl.ANY),
            pl.BlockSpec(memory_space=pl.ANY),
        ],
        out_specs=pl.BlockSpec(memory_space=pl.ANY),
        scratch_shapes=[pltpu.SemaphoreType.DMA],
        name="pick",
    )(requests, key_mem, value_mem)


def softmax_dot(scores, value):
    top = jnp.max(scores, axis=1, keepdims=True)
    raised = jnp.exp2((scores - top) * SCALE2)
    total = jnp.sum(raised, axis=1, keepdims=True)
    out = jnp.dot(raised.astype(jnp.bfloat16), value, preferred_element_type=jnp.float32)
    return out / total


def scores_of(query, key):
    return lax.dot_general(query, key, (((1,), (1,)), ((), ())), preferred_element_type=jnp.float32)


def band_kernel(q_ref, k0, k1, k2, k3, v0, v1, v2, v3, out_ref):
    rows = q_ref.shape[0]
    position = lax.axis_index("blk")
    first = (BEHIND - position) * rows
    key = jnp.concatenate([k0[...], k1[...], k2[...], k3[...]], axis=0)
    value = jnp.concatenate([v0[...], v1[...], v2[...], v3[...]], axis=0)
    width = BEHIND * rows + QBLK
    for tile in range(rows // QBLK):
        base = tile * QBLK
        scores = scores_of(q_ref[base : base + QBLK, :], key[base : base + width, :])
        row = lax.broadcasted_iota(jnp.int32, scores.shape, 0)
        col = lax.broadcasted_iota(jnp.int32, scores.shape, 1)
        allowed = (col >= jnp.maximum(row, first - base)) & (col <= row + BEHIND * rows)
        scores = jnp.where(allowed, scores, LOW)
        out_ref[base : base + QBLK, :] = softmax_dot(scores, value[base : base + width, :])


def band(queries, key_parts, value_parts):
    rows, width = queries.shape
    spec = pl.BlockSpec((rows, DH), lambda h: (0, h))
    return pl.pallas_call(
        band_kernel,
        grid=(H,),
        out_shape=jax.ShapeDtypeStruct((rows, width), jnp.float32),
        in_specs=[spec] * 9,
        out_specs=spec,
        cost_estimate=pl.CostEstimate(
            flops=2 * 2 * rows * 1024 * width, bytes_accessed=rows * width * 24, transcendentals=rows * 1024 * H
        ),
        name="band",
    )(queries, *key_parts, *value_parts)


def memory_kernel(arrival_ref, gate_ref, q_ref, band_ref, *refs):
    blocks, out_ref = refs[:-1], refs[-1]
    share = gate_ref[pl.program_id(0)]
    for tile in range(len(blocks) // RET):
        part = blocks[tile * RET : (tile + 1) * RET]
        base = tile * QBLK
        key = jnp.concatenate([b[0, 0] for b in part], axis=0)
        value = jnp.concatenate([b[0, 1] for b in part], axis=0)
        memory_out = softmax_dot(scores_of(q_ref[base : base + QBLK, :], key), value)
        mixed = share * memory_out + (1.0 - share) * band_ref[base : base + QBLK, :]
        out_ref[base : base + QBLK, :] = mixed.astype(out_ref.dtype)


def memory(arrival, gate_share, queries, band_out, arrived):
    rows, width = queries.shape
    spec = pl.BlockSpec((rows, DH), lambda h, a, g: (0, h))

    def block_spec(tile, j):
        return pl.BlockSpec((1, 2, MB, DH), lambda h, a, g: (a[(tile * H + h) * RET + j], 0, 0, 0))

    picked = [block_spec(t, j) for t in range(rows // QBLK) for j in range(RET)]
    return pl.pallas_call(
        memory_kernel,
        grid_spec=pltpu.PrefetchScalarGridSpec(
            num_scalar_prefetch=2,
            grid=(H,),
            in_specs=[spec, spec] + picked,
            out_specs=spec,
        ),
        out_shape=jax.ShapeDtypeStruct((rows, width), jnp.bfloat16),
        name="memory",
    )(arrival, gate_share, queries, band_out, *([arrived] * len(picked)))


def plan_requests(target, local_code, peer_count, peer_slots):
    request_count = target.shape[0]
    order = jnp.arange(request_count, dtype=jnp.int32)
    same_target = (target[:, None] == target[None, :]) & (order[None, :] < order[:, None])
    slot_rank = jnp.sum(same_target.astype(jnp.int32), axis=1)
    arrival = target * peer_slots + slot_rank
    places = jnp.arange(peer_count * peer_slots, dtype=jnp.int32)
    hit = places[:, None] == arrival[None, :]
    requests = jnp.sum(jnp.where(hit, local_code[None, :], 0), axis=1)
    return requests.reshape(peer_count, peer_slots), arrival


def local(queries, keys, values, memory_keys, memory_values, owners, slots, gate_logit):
    target = owners.reshape(-1)
    head_flat = jnp.broadcast_to(jnp.arange(H, dtype=jnp.int32)[None, :, None], owners.shape).reshape(-1)
    peer_count = lax.axis_size("grp") * lax.axis_size("blk")
    capacity = max(2, 5 * target.shape[0] // (4 * peer_count))
    requests, arrival = plan_requests(target, slots.reshape(-1) * H + head_flat, peer_count, capacity)
    named = lax.all_to_all(requests, ("grp", "blk"), split_axis=0, concat_axis=0, tiled=True)
    picked = pick(named.reshape(-1), memory_keys, memory_values)
    picked = picked.reshape(peer_count, capacity, 2, MB, DH)
    arrived = lax.all_to_all(picked, ("grp", "blk"), split_axis=0, concat_axis=0, tiled=True)
    arrived = arrived.reshape(peer_count * capacity, 2, MB, DH)
    key_parts = [from_behind(keys, "blk", d) for d in range(BEHIND, 0, -1)] + [keys]
    value_parts = [from_behind(values, "blk", d) for d in range(BEHIND, 0, -1)] + [values]
    band_out = band(queries, key_parts, value_parts)
    return memory(arrival, jax.nn.sigmoid(gate_logit), queries, band_out, arrived)


def solution(mesh):
    rows = P(("grp", "blk"), None)
    blocks = P(("grp", "blk"), None, None)
    return jax.shard_map(
        local,
        mesh=mesh,
        in_specs=(rows, rows, rows, blocks, blocks, blocks, blocks, P()),
        out_specs=rows,
        check_vma=False,
    )
```

```python
import functools
import math

import jax
import jax.numpy as jnp
from jax import lax
from jax.experimental import pallas as pl
from jax.experimental.pallas import tpu as pltpu
from jax.sharding import PartitionSpec as P

H = 16
QBLK = 128
MB = 64
RET = 8
DH = 128
BEHIND = 3
LOG2E = 1.4426950408889634
SCALE2 = LOG2E / math.sqrt(DH)
LOW = -1e30


def from_behind(value, axis, steps):
    count = lax.axis_size(axis)
    return lax.ppermute(value, axis, [(i, i + steps) for i in range(count - steps)])


def pick_kernel(req_ref, key_ref, value_ref, out_ref, held, sems, out_sem, *, peers, each):
    def fetch(p, carry):
        for r in range(each):
            code = jnp.maximum(req_ref[p * each + r], 0)
            block = code // H
            col = pl.multiple_of((code % H) * DH, DH)
            pltpu.make_async_copy(key_ref.at[block, :, pl.ds(col, DH)], held.at[p, r, 0], sems.at[p]).start()
            pltpu.make_async_copy(value_ref.at[block, :, pl.ds(col, DH)], held.at[p, r, 1], sems.at[p]).start()
        return carry

    def write(p, carry):
        pltpu.make_async_copy(held.at[p], held.at[p], sems.at[p]).wait()
        pltpu.make_async_copy(held.at[p], out_ref.at[p], out_sem).start()
        return carry

    lax.fori_loop(0, peers, fetch, 0)
    lax.fori_loop(0, peers, write, 0)
    pltpu.make_async_copy(held, out_ref, out_sem).wait()


def pick(requests, key_mem, value_mem, peers):
    each = requests.shape[0] // peers
    shape = (peers, each, 2, MB, DH)
    return pl.pallas_call(
        functools.partial(pick_kernel, peers=peers, each=each),
        out_shape=jax.ShapeDtypeStruct(shape, key_mem.dtype),
        in_specs=[
            pl.BlockSpec(memory_space=pltpu.SMEM),
            pl.BlockSpec(memory_space=pl.ANY),
            pl.BlockSpec(memory_space=pl.ANY),
        ],
        out_specs=pl.BlockSpec(memory_space=pl.ANY),
        scratch_shapes=[
            pltpu.VMEM(shape, key_mem.dtype),
            pltpu.SemaphoreType.DMA((peers,)),
            pltpu.SemaphoreType.DMA,
        ],
        compiler_params=pltpu.CompilerParams(vmem_limit_bytes=32 << 20),
        name="pick",
    )(requests, key_mem, value_mem)


def softmax_dot(scores, value):
    top = jnp.max(scores, axis=1, keepdims=True)
    raised = jnp.exp2((scores - top) * SCALE2)
    total = jnp.sum(raised, axis=1, keepdims=True)
    out = jnp.dot(raised.astype(jnp.bfloat16), value, preferred_element_type=jnp.float32)
    return out / total


def scores_of(query, key):
    return lax.dot_general(query, key, (((1,), (1,)), ((), ())), preferred_element_type=jnp.float32)


def band_kernel(q_ref, k0, k1, k2, k3, v0, v1, v2, v3, out_ref):
    rows = q_ref.shape[0]
    position = lax.axis_index("blk")
    first = (BEHIND - position) * rows
    key = jnp.concatenate([k0[...], k1[...], k2[...], k3[...]], axis=0)
    value = jnp.concatenate([v0[...], v1[...], v2[...], v3[...]], axis=0)
    width = BEHIND * rows + QBLK
    for tile in range(rows // QBLK):
        base = tile * QBLK
        scores = scores_of(q_ref[base : base + QBLK, :], key[base : base + width, :])
        row = lax.broadcasted_iota(jnp.int32, scores.shape, 0)
        col = lax.broadcasted_iota(jnp.int32, scores.shape, 1)
        allowed = (col >= jnp.maximum(row, first - base)) & (col <= row + BEHIND * rows)
        scores = jnp.where(allowed, scores, LOW)
        out_ref[base : base + QBLK, :] = softmax_dot(scores, value[base : base + width, :])


def band(queries, key_parts, value_parts):
    rows, width = queries.shape
    spec = pl.BlockSpec((rows, DH), lambda h: (0, h))
    return pl.pallas_call(
        band_kernel,
        grid=(H,),
        out_shape=jax.ShapeDtypeStruct((rows, width), jnp.float32),
        in_specs=[spec] * 9,
        out_specs=spec,
        cost_estimate=pl.CostEstimate(
            flops=2 * 2 * rows * 1024 * width, bytes_accessed=rows * width * 24, transcendentals=rows * 1024 * H
        ),
        name="band",
    )(queries, *key_parts, *value_parts)


def memory_kernel(arrival_ref, gate_ref, q_ref, band_ref, *refs):
    blocks, out_ref = refs[:-1], refs[-1]
    share = gate_ref[pl.program_id(0)]
    for tile in range(len(blocks) // RET):
        part = blocks[tile * RET : (tile + 1) * RET]
        base = tile * QBLK
        key = jnp.concatenate([b[0, 0] for b in part], axis=0)
        value = jnp.concatenate([b[0, 1] for b in part], axis=0)
        memory_out = softmax_dot(scores_of(q_ref[base : base + QBLK, :], key), value)
        mixed = share * memory_out + (1.0 - share) * band_ref[base : base + QBLK, :]
        out_ref[base : base + QBLK, :] = mixed.astype(out_ref.dtype)


def memory(arrival, gate_share, queries, band_out, arrived):
    rows, width = queries.shape
    spec = pl.BlockSpec((rows, DH), lambda h, a, g: (0, h))

    def block_spec(tile, j):
        return pl.BlockSpec((1, 2, MB, DH), lambda h, a, g: (a[(tile * H + h) * RET + j], 0, 0, 0))

    picked = [block_spec(t, j) for t in range(rows // QBLK) for j in range(RET)]
    return pl.pallas_call(
        memory_kernel,
        grid_spec=pltpu.PrefetchScalarGridSpec(
            num_scalar_prefetch=2,
            grid=(H,),
            in_specs=[spec, spec] + picked,
            out_specs=spec,
        ),
        out_shape=jax.ShapeDtypeStruct((rows, width), jnp.bfloat16),
        name="memory",
    )(arrival, gate_share, queries, band_out, *([arrived] * len(picked)))


def plan_requests(target, local_code, peer_count, peer_slots):
    request_count = target.shape[0]
    order = jnp.arange(request_count, dtype=jnp.int32)
    same_target = (target[:, None] == target[None, :]) & (order[None, :] < order[:, None])
    slot_rank = jnp.sum(same_target.astype(jnp.int32), axis=1)
    arrival = target * peer_slots + slot_rank
    places = jnp.arange(peer_count * peer_slots, dtype=jnp.int32)
    hit = places[:, None] == arrival[None, :]
    requests = jnp.sum(jnp.where(hit, local_code[None, :], 0), axis=1)
    return requests.reshape(peer_count, peer_slots), arrival


def local(queries, keys, values, memory_keys, memory_values, owners, slots, gate_logit):
    target = owners.reshape(-1)
    head_flat = jnp.broadcast_to(jnp.arange(H, dtype=jnp.int32)[None, :, None], owners.shape).reshape(-1)
    peer_count = lax.axis_size("grp") * lax.axis_size("blk")
    capacity = max(2, 5 * target.shape[0] // (4 * peer_count))
    requests, arrival = plan_requests(target, slots.reshape(-1) * H + head_flat, peer_count, capacity)
    named = lax.all_to_all(requests, ("grp", "blk"), split_axis=0, concat_axis=0, tiled=True)
    picked = pick(named.reshape(-1), memory_keys, memory_values, peer_count)
    arrived = lax.all_to_all(picked, ("grp", "blk"), split_axis=0, concat_axis=0, tiled=True)
    arrived = arrived.reshape(peer_count * capacity, 2, MB, DH)
    key_parts = [from_behind(keys, "blk", d) for d in range(BEHIND, 0, -1)] + [keys]
    value_parts = [from_behind(values, "blk", d) for d in range(BEHIND, 0, -1)] + [values]
    band_out = band(queries, key_parts, value_parts)
    return memory(arrival, jax.nn.sigmoid(gate_logit), queries, band_out, arrived)


def solution(mesh):
    rows = P(("grp", "blk"), None)
    blocks = P(("grp", "blk"), None, None)
    return jax.shard_map(
        local,
        mesh=mesh,
        in_specs=(rows, rows, rows, blocks, blocks, blocks, blocks, P()),
        out_specs=rows,
        check_vma=False,
    )
```

```python
import functools
import math

import jax
import jax.numpy as jnp
from jax import lax
from jax.experimental import pallas as pl
from jax.experimental.pallas import tpu as pltpu
from jax.sharding import PartitionSpec as P

H = 16
QBLK = 128
MB = 64
RET = 8
DH = 128
BEHIND = 3
GROUP = BEHIND + 1
LOG2E = 1.4426950408889634
SCALE2 = LOG2E / math.sqrt(DH)
LOW = -1e30


def from_behind(value, axis, steps):
    count = lax.axis_size(axis)
    return lax.ppermute(value, axis, [(i, i + steps) for i in range(count - steps)])


def pick_kernel(req_ref, key_ref, value_ref, out_ref, held, sems, out_sem, *, peers, each):
    def fetch(p, carry):
        for r in range(each):
            code = jnp.maximum(req_ref[p * each + r], 0)
            block = code // H
            col = pl.multiple_of((code % H) * DH, DH)
            pltpu.make_async_copy(key_ref.at[block, :, pl.ds(col, DH)], held.at[p, r, 0], sems.at[p]).start()
            pltpu.make_async_copy(value_ref.at[block, :, pl.ds(col, DH)], held.at[p, r, 1], sems.at[p]).start()
        return carry

    def write(p, carry):
        pltpu.make_async_copy(held.at[p], held.at[p], sems.at[p]).wait()
        pltpu.make_async_copy(held.at[p], out_ref.at[p], out_sem).start()
        return carry

    lax.fori_loop(0, peers, fetch, 0)
    lax.fori_loop(0, peers, write, 0)
    pltpu.make_async_copy(held, out_ref, out_sem).wait()


def pick(requests, key_mem, value_mem, peers):
    each = requests.shape[0] // peers
    shape = (peers, each, 2, MB, DH)
    return pl.pallas_call(
        functools.partial(pick_kernel, peers=peers, each=each),
        out_shape=jax.ShapeDtypeStruct(shape, key_mem.dtype),
        in_specs=[
            pl.BlockSpec(memory_space=pltpu.SMEM),
            pl.BlockSpec(memory_space=pl.ANY),
            pl.BlockSpec(memory_space=pl.ANY),
        ],
        out_specs=pl.BlockSpec(memory_space=pl.ANY),
        scratch_shapes=[
            pltpu.VMEM(shape, key_mem.dtype),
            pltpu.SemaphoreType.DMA((peers,)),
            pltpu.SemaphoreType.DMA,
        ],
        compiler_params=pltpu.CompilerParams(vmem_limit_bytes=56 << 20),
        name="pick",
    )(requests, key_mem, value_mem)


def softmax_dot(scores, value):
    top = jnp.max(scores, axis=1, keepdims=True)
    raised = jnp.exp2((scores - top) * SCALE2)
    total = jnp.sum(raised, axis=1, keepdims=True)
    out = jnp.dot(raised.astype(jnp.bfloat16), value, preferred_element_type=jnp.float32)
    return out / total


def scores_of(query, key):
    return lax.dot_general(query, key, (((1,), (1,)), ((), ())), preferred_element_type=jnp.float32)


def band_kernel(q_ref, key_ref, value_ref, key_before, value_before, out_ref):
    rows = q_ref.shape[2]
    behind = BEHIND * rows
    place = lax.axis_index("blk")
    first = jnp.where(place < GROUP, behind, 0)
    key = jnp.concatenate([key_before[...].reshape(behind, DH), key_ref[...].reshape(GROUP * rows, DH)], axis=0)
    value = jnp.concatenate([value_before[...].reshape(behind, DH), value_ref[...].reshape(GROUP * rows, DH)], axis=0)
    width = behind + QBLK
    for tile in range(GROUP * rows // QBLK):
        base = tile * QBLK
        member, start = divmod(base, rows)
        scores = scores_of(q_ref[member, 0, start : start + QBLK, :], key[base : base + width, :])
        row = lax.broadcasted_iota(jnp.int32, scores.shape, 0)
        col = lax.broadcasted_iota(jnp.int32, scores.shape, 1)
        allowed = (col >= jnp.maximum(row, first - base)) & (col <= row + behind)
        scores = jnp.where(allowed, scores, LOW)
        result = softmax_dot(scores, value[base : base + width, :])
        shift = (member - place % GROUP + GROUP) % GROUP
        out_ref[shift, start : start + QBLK, :] = result.astype(out_ref.dtype)


def band(gathered, before):
    members, _, rows, width = gathered.shape

    def spec(which):
        return pl.BlockSpec((members, 1, rows, DH), lambda h: (0, which, 0, h))

    def spec_before(which):
        return pl.BlockSpec((BEHIND, 1, rows, DH), lambda h: (0, which, 0, h))

    return pl.pallas_call(
        band_kernel,
        grid=(width // DH,),
        out_shape=jax.ShapeDtypeStruct((members, rows, width), jnp.bfloat16),
        in_specs=[spec(0), spec(1), spec(2), spec_before(0), spec_before(1)],
        out_specs=pl.BlockSpec((members, rows, DH), lambda h: (0, 0, h)),
        cost_estimate=pl.CostEstimate(
            flops=2 * 2 * members * rows * 1024 * width,
            bytes_accessed=members * rows * width * 14,
            transcendentals=members * rows * 1024 * width // DH,
        ),
        compiler_params=pltpu.CompilerParams(vmem_limit_bytes=56 << 20),
        name="band",
    )(gathered, gathered, gathered, before, before)


def pack_kernel(q_ref, k_ref, v_ref, out_ref):
    out_ref[0, 0] = q_ref[...]
    out_ref[0, 1] = k_ref[...]
    out_ref[0, 2] = v_ref[...]


def pack(queries, keys, values):
    rows, width = queries.shape
    part = width // GROUP
    spec = pl.BlockSpec((rows, part), lambda g: (0, g))
    return pl.pallas_call(
        pack_kernel,
        grid=(GROUP,),
        out_shape=jax.ShapeDtypeStruct((GROUP, 3, rows, part), queries.dtype),
        in_specs=[spec] * 3,
        out_specs=pl.BlockSpec((1, 3, rows, part), lambda g: (g, 0, 0, 0)),
        compiler_params=pltpu.CompilerParams(vmem_limit_bytes=56 << 20),
        name="pack",
    )(queries, keys, values)


def gather_heads(queries, keys, values):
    count = lax.axis_size("blk")
    groups = [[g + i for i in range(GROUP)] for g in range(0, count, GROUP)]
    gathered = lax.all_to_all(
        pack(queries, keys, values),
        "blk",
        split_axis=0,
        concat_axis=0,
        axis_index_groups=groups,
        tiled=True,
    )
    return gathered, from_behind(gathered[GROUP - BEHIND :, 1:], "blk", GROUP)


def return_rows(parts):
    count = lax.axis_size("blk")
    back = [parts[0]]
    for shift in range(1, GROUP):
        pairs = [(i, i // GROUP * GROUP + (i + shift) % GROUP) for i in range(count)]
        back.append(lax.ppermute(parts[shift], "blk", pairs))
    return jnp.stack(back)


def memory_kernel(arrival_ref, gate_ref, q_ref, band_ref, *refs):
    blocks, out_ref = refs[:-1], refs[-1]
    share = gate_ref[pl.program_id(0)]
    for tile in range(len(blocks) // RET):
        part = blocks[tile * RET : (tile + 1) * RET]
        base = tile * QBLK
        key = jnp.concatenate([b[0, 0] for b in part], axis=0)
        value = jnp.concatenate([b[0, 1] for b in part], axis=0)
        memory_out = softmax_dot(scores_of(q_ref[base : base + QBLK, :], key), value)
        mixed = share * memory_out + (1.0 - share) * band_ref[0, base : base + QBLK, :].astype(jnp.float32)
        out_ref[base : base + QBLK, :] = mixed.astype(out_ref.dtype)


def memory(arrival, gate_share, queries, band_out, arrived):
    rows, width = queries.shape
    spec = pl.BlockSpec((rows, DH), lambda h, a, g: (0, h))

    each = H // GROUP
    last = arrival.shape[0] - 1
    band_spec = pl.BlockSpec((1, rows, DH), lambda h, a, g: ((a[last] - h // each + GROUP) % GROUP, 0, h % each))

    def block_spec(tile, j):
        return pl.BlockSpec((1, 2, MB, DH), lambda h, a, g: (a[(tile * H + h) * RET + j], 0, 0, 0))

    picked = [block_spec(t, j) for t in range(rows // QBLK) for j in range(RET)]
    return pl.pallas_call(
        memory_kernel,
        grid_spec=pltpu.PrefetchScalarGridSpec(
            num_scalar_prefetch=2,
            grid=(H,),
            in_specs=[spec, band_spec] + picked,
            out_specs=spec,
        ),
        out_shape=jax.ShapeDtypeStruct((rows, width), jnp.bfloat16),
        name="memory",
    )(arrival, gate_share, queries, band_out, *([arrived] * len(picked)))


def plan_requests(target, local_code, peer_count, peer_slots):
    request_count = target.shape[0]
    order = jnp.arange(request_count, dtype=jnp.int32)
    same_target = (target[:, None] == target[None, :]) & (order[None, :] < order[:, None])
    slot_rank = jnp.sum(same_target.astype(jnp.int32), axis=1)
    arrival = target * peer_slots + slot_rank
    places = jnp.arange(peer_count * peer_slots, dtype=jnp.int32)
    hit = places[:, None] == arrival[None, :]
    requests = jnp.sum(jnp.where(hit, local_code[None, :], 0), axis=1)
    return requests.reshape(peer_count, peer_slots), arrival


def local(queries, keys, values, memory_keys, memory_values, owners, slots, gate_logit):
    target = owners.reshape(-1)
    head_flat = jnp.broadcast_to(jnp.arange(H, dtype=jnp.int32)[None, :, None], owners.shape).reshape(-1)
    peer_count = lax.axis_size("grp") * lax.axis_size("blk")
    capacity = max(2, 5 * target.shape[0] // (4 * peer_count))
    requests, arrival = plan_requests(target, slots.reshape(-1) * H + head_flat, peer_count, capacity)
    named = lax.all_to_all(requests, ("grp", "blk"), split_axis=0, concat_axis=0, tiled=True)
    gathered, before = gather_heads(queries, keys, values)
    named, before = lax.optimization_barrier((named, before))
    picked = pick(named.reshape(-1), memory_keys, memory_values, peer_count)
    arrived = lax.all_to_all(picked, ("grp", "blk"), split_axis=0, concat_axis=0, tiled=True)
    arrived = arrived.reshape(peer_count * capacity, 2, MB, DH)
    band_out = return_rows(band(gathered, before))
    member = lax.axis_index("blk") % GROUP
    arrival = jnp.concatenate([arrival, member[None].astype(jnp.int32)])
    return memory(arrival, jax.nn.sigmoid(gate_logit), queries, band_out, arrived)


def solution(mesh):
    rows = P(("grp", "blk"), None)
    blocks = P(("grp", "blk"), None, None)
    return jax.shard_map(
        local,
        mesh=mesh,
        in_specs=(rows, rows, rows, blocks, blocks, blocks, blocks, P()),
        out_specs=rows,
        check_vma=False,
    )
```

```python
import functools
import math

import jax
import jax.numpy as jnp
from jax import lax
from jax.experimental import pallas as pl
from jax.experimental.pallas import tpu as pltpu
from jax.sharding import PartitionSpec as P

H = 16
QBLK = 128
MB = 64
RET = 8
DH = 128
BEHIND = 3
GROUP = BEHIND + 1
LOG2E = 1.4426950408889634
SCALE2 = LOG2E / math.sqrt(DH)
LOW = -1e30


def from_behind(value, axis, steps):
    count = lax.axis_size(axis)
    return lax.ppermute(value, axis, [(i, i + steps) for i in range(count - steps)])


def pick_kernel(req_ref, key_ref, value_ref, out_ref, held, sems, out_sem, *, peers, each):
    def fetch(p, carry):
        for r in range(each):
            code = jnp.maximum(req_ref[p * each + r], 0)
            block = code // H
            col = pl.multiple_of((code % H) * DH, DH)
            pltpu.make_async_copy(key_ref.at[block, :, pl.ds(col, DH)], held.at[p, r, 0], sems.at[p]).start()
            pltpu.make_async_copy(value_ref.at[block, :, pl.ds(col, DH)], held.at[p, r, 1], sems.at[p]).start()
        return carry

    def write(p, carry):
        pltpu.make_async_copy(held.at[p], held.at[p], sems.at[p]).wait()
        pltpu.make_async_copy(held.at[p], out_ref.at[p], out_sem).start()
        return carry

    lax.fori_loop(0, peers, fetch, 0)
    lax.fori_loop(0, peers, write, 0)
    pltpu.make_async_copy(held, out_ref, out_sem).wait()


def pick(requests, key_mem, value_mem, peers):
    each = requests.shape[0] // peers
    shape = (peers, each, 2, MB, DH)
    return pl.pallas_call(
        functools.partial(pick_kernel, peers=peers, each=each),
        out_shape=jax.ShapeDtypeStruct(shape, key_mem.dtype),
        in_specs=[
            pl.BlockSpec(memory_space=pltpu.SMEM),
            pl.BlockSpec(memory_space=pl.ANY),
            pl.BlockSpec(memory_space=pl.ANY),
        ],
        out_specs=pl.BlockSpec(memory_space=pl.ANY),
        scratch_shapes=[
            pltpu.VMEM(shape, key_mem.dtype),
            pltpu.SemaphoreType.DMA((peers,)),
            pltpu.SemaphoreType.DMA,
        ],
        compiler_params=pltpu.CompilerParams(vmem_limit_bytes=56 << 20),
        name="pick",
    )(requests, key_mem, value_mem)


def softmax_dot(scores, value):
    top = jnp.max(scores, axis=1, keepdims=True)
    raised = jnp.exp2((scores - top) * SCALE2)
    total = jnp.sum(raised, axis=1, keepdims=True)
    out = jnp.dot(raised.astype(jnp.bfloat16), value, preferred_element_type=jnp.float32)
    return out / total


def scores_of(query, key):
    return lax.dot_general(query, key, (((1,), (1,)), ((), ())), preferred_element_type=jnp.float32)


def band_kernel(*refs):
    own, before = refs[:GROUP], refs[GROUP : 2 * GROUP]
    out_ref, query, key, value = refs[2 * GROUP :]
    rows = query.shape[1]
    behind = BEHIND * rows
    place = lax.axis_index("blk")
    first = jnp.where(place < GROUP, behind, 0)
    for shift in range(GROUP):
        source = (place % GROUP - shift + GROUP) % GROUP
        at = pl.multiple_of(behind + source * rows, rows)
        query[source] = own[shift][0]
        key[pl.ds(at, rows), :] = own[shift][1]
        value[pl.ds(at, rows), :] = own[shift][2]

        @pl.when(source >= GROUP - BEHIND)
        def _():
            earlier = pl.multiple_of((source - (GROUP - BEHIND)) * rows, rows)
            key[pl.ds(earlier, rows), :] = before[shift][0]
            value[pl.ds(earlier, rows), :] = before[shift][1]

    width = behind + QBLK
    for tile in range(GROUP * rows // QBLK):
        base = tile * QBLK
        member, start = divmod(base, rows)
        scores = scores_of(query[member, start : start + QBLK, :], key[base : base + width, :])
        row = lax.broadcasted_iota(jnp.int32, scores.shape, 0)
        col = lax.broadcasted_iota(jnp.int32, scores.shape, 1)
        allowed = (col >= jnp.maximum(row, first - base)) & (col <= row + behind)
        scores = jnp.where(allowed, scores, LOW)
        result = softmax_dot(scores, value[base : base + width, :])
        shift = (member - place % GROUP + GROUP) % GROUP
        out_ref[shift, start : start + QBLK, :] = result.astype(out_ref.dtype)


def band(own, before):
    _, rows, width = own[0].shape
    return pl.pallas_call(
        band_kernel,
        grid=(width // DH,),
        out_shape=jax.ShapeDtypeStruct((GROUP, rows, width), jnp.bfloat16),
        in_specs=[pl.BlockSpec((3, rows, DH), lambda h: (0, 0, h))] * GROUP
        + [pl.BlockSpec((2, rows, DH), lambda h: (0, 0, h))] * GROUP,
        out_specs=pl.BlockSpec((GROUP, rows, DH), lambda h: (0, 0, h)),
        scratch_shapes=[
            pltpu.VMEM((GROUP, rows, DH), jnp.bfloat16),
            pltpu.VMEM(((GROUP + BEHIND) * rows, DH), jnp.bfloat16),
            pltpu.VMEM(((GROUP + BEHIND) * rows, DH), jnp.bfloat16),
        ],
        cost_estimate=pl.CostEstimate(
            flops=2 * 2 * GROUP * rows * 1024 * width,
            bytes_accessed=GROUP * rows * width * 14,
            transcendentals=GROUP * rows * 1024 * width // DH,
        ),
        compiler_params=pltpu.CompilerParams(vmem_limit_bytes=56 << 20),
        name="band",
    )(*own, *before)


def pack_kernel(member_ref, q_ref, k_ref, v_ref, out_ref):
    out_ref[0, 0] = q_ref[...]
    out_ref[0, 1] = k_ref[...]
    out_ref[0, 2] = v_ref[...]


def pack(member, queries, keys, values):
    rows, width = queries.shape
    part = width // GROUP
    spec = pl.BlockSpec((rows, part), lambda s, m: (0, (m[0] + s) % GROUP))
    return pl.pallas_call(
        pack_kernel,
        grid_spec=pltpu.PrefetchScalarGridSpec(
            num_scalar_prefetch=1,
            grid=(GROUP,),
            in_specs=[spec] * 3,
            out_specs=pl.BlockSpec((1, 3, rows, part), lambda s, m: (s, 0, 0, 0)),
        ),
        out_shape=jax.ShapeDtypeStruct((GROUP, 3, rows, part), queries.dtype),
        compiler_params=pltpu.CompilerParams(vmem_limit_bytes=56 << 20),
        name="pack",
    )(member, queries, keys, values)


def share_heads(packed):
    count = lax.axis_size("blk")

    def target(i, shift):
        return i // GROUP * GROUP + (i + shift) % GROUP

    before = []
    for shift in range(GROUP):
        pairs = [
            (i, target(i, shift) + GROUP) for i in range(count - GROUP) if i % GROUP >= GROUP - BEHIND
        ]
        before.append(lax.ppermute(packed[shift, 1:], "blk", pairs))
    own = [packed[0]]
    for shift in range(1, GROUP):
        own.append(lax.ppermute(packed[shift], "blk", [(i, target(i, shift)) for i in range(count)]))
    return own, before


def return_rows(parts):
    count = lax.axis_size("blk")
    back = [parts[0]]
    for shift in range(1, GROUP):
        pairs = [(i, i // GROUP * GROUP + (i + shift) % GROUP) for i in range(count)]
        back.append(lax.ppermute(parts[shift], "blk", pairs))
    return jnp.stack(back)


def memory_kernel(arrival_ref, gate_ref, q_ref, band_ref, *refs):
    blocks, out_ref = refs[:-1], refs[-1]
    share = gate_ref[pl.program_id(0)]
    for tile in range(len(blocks) // RET):
        part = blocks[tile * RET : (tile + 1) * RET]
        base = tile * QBLK
        key = jnp.concatenate([b[0, 0] for b in part], axis=0)
        value = jnp.concatenate([b[0, 1] for b in part], axis=0)
        memory_out = softmax_dot(scores_of(q_ref[base : base + QBLK, :], key), value)
        mixed = share * memory_out + (1.0 - share) * band_ref[0, base : base + QBLK, :].astype(jnp.float32)
        out_ref[base : base + QBLK, :] = mixed.astype(out_ref.dtype)


def memory(arrival, gate_share, queries, band_out, arrived):
    rows, width = queries.shape
    spec = pl.BlockSpec((rows, DH), lambda h, a, g: (0, h))

    each = H // GROUP
    last = arrival.shape[0] - 1
    band_spec = pl.BlockSpec((1, rows, DH), lambda h, a, g: ((a[last] - h // each + GROUP) % GROUP, 0, h % each))

    def block_spec(tile, j):
        return pl.BlockSpec((1, 2, MB, DH), lambda h, a, g: (a[(tile * H + h) * RET + j], 0, 0, 0))

    picked = [block_spec(t, j) for t in range(rows // QBLK) for j in range(RET)]
    return pl.pallas_call(
        memory_kernel,
        grid_spec=pltpu.PrefetchScalarGridSpec(
            num_scalar_prefetch=2,
            grid=(H,),
            in_specs=[spec, band_spec] + picked,
            out_specs=spec,
        ),
        out_shape=jax.ShapeDtypeStruct((rows, width), jnp.bfloat16),
        name="memory",
    )(arrival, gate_share, queries, band_out, *([arrived] * len(picked)))


def plan_requests(target, local_code, peer_count, peer_slots):
    request_count = target.shape[0]
    order = jnp.arange(request_count, dtype=jnp.int32)
    same_target = (target[:, None] == target[None, :]) & (order[None, :] < order[:, None])
    slot_rank = jnp.sum(same_target.astype(jnp.int32), axis=1)
    arrival = target * peer_slots + slot_rank
    places = jnp.arange(peer_count * peer_slots, dtype=jnp.int32)
    hit = places[:, None] == arrival[None, :]
    requests = jnp.sum(jnp.where(hit, local_code[None, :], 0), axis=1)
    return requests.reshape(peer_count, peer_slots), arrival


def local(queries, keys, values, memory_keys, memory_values, owners, slots, gate_logit):
    target = owners.reshape(-1)
    head_flat = jnp.broadcast_to(jnp.arange(H, dtype=jnp.int32)[None, :, None], owners.shape).reshape(-1)
    peer_count = lax.axis_size("grp") * lax.axis_size("blk")
    capacity = max(2, 5 * target.shape[0] // (4 * peer_count))
    requests, arrival = plan_requests(target, slots.reshape(-1) * H + head_flat, peer_count, capacity)
    member = (lax.axis_index("blk") % GROUP).astype(jnp.int32)[None]
    packed = pack(member, queries, keys, values)
    requests, packed = lax.optimization_barrier((requests, packed))
    own, before = share_heads(packed)
    named = lax.all_to_all(requests, ("grp", "blk"), split_axis=0, concat_axis=0, tiled=True)
    picked = pick(named.reshape(-1), memory_keys, memory_values, peer_count)
    picked, own, before = lax.optimization_barrier((picked, own, before))
    arrived = lax.all_to_all(picked, ("grp", "blk"), split_axis=0, concat_axis=0, tiled=True)
    arrived = arrived.reshape(peer_count * capacity, 2, MB, DH)
    band_out = return_rows(band(own, before))
    arrival = jnp.concatenate([arrival, member])
    return memory(arrival, jax.nn.sigmoid(gate_logit), queries, band_out, arrived)


def solution(mesh):
    rows = P(("grp", "blk"), None)
    blocks = P(("grp", "blk"), None, None)
    return jax.shard_map(
        local,
        mesh=mesh,
        in_specs=(rows, rows, rows, blocks, blocks, blocks, blocks, P()),
        out_specs=rows,
        check_vma=False,
    )
```

```python
import functools
import math

import jax
import jax.numpy as jnp
from jax import lax
from jax.experimental import pallas as pl
from jax.experimental.pallas import tpu as pltpu
from jax.sharding import PartitionSpec as P

H = 16
QBLK = 128
MB = 64
RET = 8
DH = 128
BEHIND = 3
GROUP = BEHIND + 1
LOG2E = 1.4426950408889634
SCALE2 = LOG2E / math.sqrt(DH)
LOW = -1e30


def from_behind(value, axis, steps):
    count = lax.axis_size(axis)
    return lax.ppermute(value, axis, [(i, i + steps) for i in range(count - steps)])


def pick_kernel(req_ref, key_ref, value_ref, out_ref, held, sems, out_sem, *, peers, each):
    def fetch(p, carry):
        for r in range(each):
            code = jnp.maximum(req_ref[p * each + r], 0)
            block = code // H
            col = pl.multiple_of((code % H) * DH, DH)
            pltpu.make_async_copy(key_ref.at[block, :, pl.ds(col, DH)], held.at[p, r, 0], sems.at[p]).start()
            pltpu.make_async_copy(value_ref.at[block, :, pl.ds(col, DH)], held.at[p, r, 1], sems.at[p]).start()
        return carry

    def write(p, carry):
        pltpu.make_async_copy(held.at[p], held.at[p], sems.at[p]).wait()
        pltpu.make_async_copy(held.at[p], out_ref.at[p], out_sem).start()
        return carry

    lax.fori_loop(0, peers, fetch, 0)
    lax.fori_loop(0, peers, write, 0)
    pltpu.make_async_copy(held, out_ref, out_sem).wait()


def pick(requests, key_mem, value_mem, peers):
    each = requests.shape[0] // peers
    shape = (peers, each, 2, MB, DH)
    return pl.pallas_call(
        functools.partial(pick_kernel, peers=peers, each=each),
        out_shape=jax.ShapeDtypeStruct(shape, key_mem.dtype),
        in_specs=[
            pl.BlockSpec(memory_space=pltpu.SMEM),
            pl.BlockSpec(memory_space=pl.ANY),
            pl.BlockSpec(memory_space=pl.ANY),
        ],
        out_specs=pl.BlockSpec(memory_space=pl.ANY),
        scratch_shapes=[
            pltpu.VMEM(shape, key_mem.dtype),
            pltpu.SemaphoreType.DMA((peers,)),
            pltpu.SemaphoreType.DMA,
        ],
        compiler_params=pltpu.CompilerParams(vmem_limit_bytes=56 << 20),
        name="pick",
    )(requests, key_mem, value_mem)


def softmax_dot(scores, value):
    top = jnp.max(scores, axis=1, keepdims=True)
    raised = jnp.exp2((scores - top) * SCALE2)
    total = jnp.sum(raised, axis=1, keepdims=True)
    out = jnp.dot(raised.astype(jnp.bfloat16), value, preferred_element_type=jnp.float32)
    return out / total


def scores_of(query, key):
    return lax.dot_general(query, key, (((1,), (1,)), ((), ())), preferred_element_type=jnp.float32)


def band_kernel(*refs):
    own, before = refs[:GROUP], refs[GROUP : 2 * GROUP]
    out_ref, query, key, value = refs[2 * GROUP :]
    rows = query.shape[1]
    behind = BEHIND * rows
    place = lax.axis_index("blk")
    first = jnp.where(place < GROUP, behind, 0)
    for shift in range(GROUP):
        source = (place % GROUP - shift + GROUP) % GROUP
        at = pl.multiple_of(behind + source * rows, rows)
        query[source] = own[shift][0]
        key[pl.ds(at, rows), :] = own[shift][1]
        value[pl.ds(at, rows), :] = own[shift][2]

        @pl.when(source >= GROUP - BEHIND)
        def _():
            earlier = pl.multiple_of((source - (GROUP - BEHIND)) * rows, rows)
            key[pl.ds(earlier, rows), :] = before[shift][0]
            value[pl.ds(earlier, rows), :] = before[shift][1]

    width = behind + QBLK
    for tile in range(GROUP * rows // QBLK):
        base = tile * QBLK
        member, start = divmod(base, rows)
        scores = scores_of(query[member, start : start + QBLK, :], key[base : base + width, :])
        row = lax.broadcasted_iota(jnp.int32, scores.shape, 0)
        col = lax.broadcasted_iota(jnp.int32, scores.shape, 1)
        allowed = (col >= jnp.maximum(row, first - base)) & (col <= row + behind)
        scores = jnp.where(allowed, scores, LOW)
        result = softmax_dot(scores, value[base : base + width, :])
        shift = (member - place % GROUP + GROUP) % GROUP
        out_ref[shift, start : start + QBLK, :] = result.astype(out_ref.dtype)


def band(own, before):
    _, rows, width = own[0].shape
    return pl.pallas_call(
        band_kernel,
        grid=(width // DH,),
        out_shape=jax.ShapeDtypeStruct((GROUP, rows, width), jnp.bfloat16),
        in_specs=[pl.BlockSpec((3, rows, DH), lambda h: (0, 0, h))] * GROUP
        + [pl.BlockSpec((2, rows, DH), lambda h: (0, 0, h))] * GROUP,
        out_specs=pl.BlockSpec((GROUP, rows, DH), lambda h: (0, 0, h)),
        scratch_shapes=[
            pltpu.VMEM((GROUP, rows, DH), jnp.bfloat16),
            pltpu.VMEM(((GROUP + BEHIND) * rows, DH), jnp.bfloat16),
            pltpu.VMEM(((GROUP + BEHIND) * rows, DH), jnp.bfloat16),
        ],
        cost_estimate=pl.CostEstimate(
            flops=2 * 2 * GROUP * rows * 1024 * width,
            bytes_accessed=GROUP * rows * width * 14,
            transcendentals=GROUP * rows * 1024 * width // DH,
        ),
        compiler_params=pltpu.CompilerParams(vmem_limit_bytes=56 << 20),
        name="band",
    )(*own, *before)


def pack_kernel(member_ref, q_ref, k_ref, v_ref, out_ref):
    out_ref[0, 0] = q_ref[...]
    out_ref[0, 1] = k_ref[...]
    out_ref[0, 2] = v_ref[...]


def pack(member, queries, keys, values):
    rows, width = queries.shape
    part = width // GROUP
    spec = pl.BlockSpec((rows, part), lambda s, m: (0, (m[0] + s) % GROUP))
    return pl.pallas_call(
        pack_kernel,
        grid_spec=pltpu.PrefetchScalarGridSpec(
            num_scalar_prefetch=1,
            grid=(GROUP,),
            in_specs=[spec] * 3,
            out_specs=pl.BlockSpec((1, 3, rows, part), lambda s, m: (s, 0, 0, 0)),
        ),
        out_shape=jax.ShapeDtypeStruct((GROUP, 3, rows, part), queries.dtype),
        compiler_params=pltpu.CompilerParams(vmem_limit_bytes=56 << 20),
        name="pack",
    )(member, queries, keys, values)


def share_heads(packed):
    count = lax.axis_size("blk")

    def target(i, shift):
        return i // GROUP * GROUP + (i + shift) % GROUP

    before = []
    for shift in range(GROUP):
        pairs = [
            (i, target(i, shift) + GROUP) for i in range(count - GROUP) if i % GROUP >= GROUP - BEHIND
        ]
        before.append(lax.ppermute(packed[shift, 1:], "blk", pairs))
    own = [packed[0]]
    for shift in range(1, GROUP):
        own.append(lax.ppermute(packed[shift], "blk", [(i, target(i, shift)) for i in range(count)]))
    return own, before


def return_rows(parts):
    count = lax.axis_size("blk")
    back = [parts[0]]
    for shift in range(1, GROUP):
        pairs = [(i, i // GROUP * GROUP + (i + shift) % GROUP) for i in range(count)]
        back.append(lax.ppermute(parts[shift], "blk", pairs))
    return jnp.stack(back)


def memory_kernel(arrival_ref, gate_ref, q_ref, band_ref, *refs):
    blocks, out_ref = refs[:-1], refs[-1]
    share = gate_ref[pl.program_id(0)]
    for tile in range(len(blocks) // RET):
        part = blocks[tile * RET : (tile + 1) * RET]
        base = tile * QBLK
        key = jnp.concatenate([b[0, 0] for b in part], axis=0)
        value = jnp.concatenate([b[0, 1] for b in part], axis=0)
        memory_out = softmax_dot(scores_of(q_ref[base : base + QBLK, :], key), value)
        mixed = share * memory_out + (1.0 - share) * band_ref[0, base : base + QBLK, :].astype(jnp.float32)
        out_ref[base : base + QBLK, :] = mixed.astype(out_ref.dtype)


def memory(arrival, gate_share, queries, band_out, arrived):
    rows, width = queries.shape
    spec = pl.BlockSpec((rows, DH), lambda h, a, g: (0, h))

    each = H // GROUP
    last = arrival.shape[0] - 1
    band_spec = pl.BlockSpec((1, rows, DH), lambda h, a, g: ((a[last] - h // each + GROUP) % GROUP, 0, h % each))

    def block_spec(tile, j):
        return pl.BlockSpec((1, 2, MB, DH), lambda h, a, g: (a[(tile * H + h) * RET + j], 0, 0, 0))

    picked = [block_spec(t, j) for t in range(rows // QBLK) for j in range(RET)]
    return pl.pallas_call(
        memory_kernel,
        grid_spec=pltpu.PrefetchScalarGridSpec(
            num_scalar_prefetch=2,
            grid=(H,),
            in_specs=[spec, band_spec] + picked,
            out_specs=spec,
        ),
        out_shape=jax.ShapeDtypeStruct((rows, width), jnp.bfloat16),
        name="memory",
    )(arrival, gate_share, queries, band_out, *([arrived] * len(picked)))


def plan_requests(target, local_code, peer_count, peer_slots):
    request_count = target.shape[0]
    order = jnp.arange(request_count, dtype=jnp.int32)
    same_target = (target[:, None] == target[None, :]) & (order[None, :] < order[:, None])
    slot_rank = jnp.sum(same_target.astype(jnp.int32), axis=1)
    arrival = target * peer_slots + slot_rank
    places = jnp.arange(peer_count * peer_slots, dtype=jnp.int32)
    hit = places[:, None] == arrival[None, :]
    requests = jnp.sum(jnp.where(hit, local_code[None, :], 0), axis=1)
    return requests.reshape(peer_count, peer_slots), arrival


def local(queries, keys, values, memory_keys, memory_values, owners, slots, gate_logit):
    target = owners.reshape(-1)
    head_flat = jnp.broadcast_to(jnp.arange(H, dtype=jnp.int32)[None, :, None], owners.shape).reshape(-1)
    peer_count = lax.axis_size("grp") * lax.axis_size("blk")
    capacity = max(2, 5 * target.shape[0] // (4 * peer_count))
    requests, arrival = plan_requests(target, slots.reshape(-1) * H + head_flat, peer_count, capacity)
    member = (lax.axis_index("blk") % GROUP).astype(jnp.int32)[None]
    packed = pack(member, queries, keys, values)
    named = lax.all_to_all(requests, ("grp", "blk"), split_axis=0, concat_axis=0, tiled=True)
    named, packed = lax.optimization_barrier((named, packed))
    own, before = share_heads(packed)
    picked = pick(named.reshape(-1), memory_keys, memory_values, peer_count)
    arrived = lax.all_to_all(picked, ("grp", "blk"), split_axis=0, concat_axis=0, tiled=True)
    arrived = arrived.reshape(peer_count * capacity, 2, MB, DH)
    band_out = return_rows(band(own, before))
    arrival = jnp.concatenate([arrival, member])
    return memory(arrival, jax.nn.sigmoid(gate_logit), queries, band_out, arrived)


def solution(mesh):
    rows = P(("grp", "blk"), None)
    blocks = P(("grp", "blk"), None, None)
    return jax.shard_map(
        local,
        mesh=mesh,
        in_specs=(rows, rows, rows, blocks, blocks, blocks, blocks, P()),
        out_specs=rows,
        check_vma=False,
    )
```

```python
import functools
import math

import jax
import jax.numpy as jnp
from jax import lax
from jax.experimental import pallas as pl
from jax.experimental.pallas import tpu as pltpu
from jax.sharding import PartitionSpec as P

H = 16
QBLK = 128
MB = 64
RET = 8
DH = 128
BEHIND = 3
GROUP = BEHIND + 1
LOG2E = 1.4426950408889634
SCALE2 = LOG2E / math.sqrt(DH)
LOW = -1e30


def from_behind(value, axis, steps):
    count = lax.axis_size(axis)
    return lax.ppermute(value, axis, [(i, i + steps) for i in range(count - steps)])


def pick_kernel(req_ref, key_ref, value_ref, out_ref, held, sems, out_sem, *, peers, each):
    def fetch(p, carry):
        for r in range(each):
            code = jnp.maximum(req_ref[p * each + r], 0)
            block = code // H
            col = pl.multiple_of((code % H) * DH, DH)
            pltpu.make_async_copy(key_ref.at[block, :, pl.ds(col, DH)], held.at[p, r, 0], sems.at[p]).start()
            pltpu.make_async_copy(value_ref.at[block, :, pl.ds(col, DH)], held.at[p, r, 1], sems.at[p]).start()
        return carry

    def write(p, carry):
        pltpu.make_async_copy(held.at[p], held.at[p], sems.at[p]).wait()
        pltpu.make_async_copy(held.at[p], out_ref.at[p], out_sem).start()
        return carry

    lax.fori_loop(0, peers, fetch, 0)
    lax.fori_loop(0, peers, write, 0)
    pltpu.make_async_copy(held, out_ref, out_sem).wait()


def pick(requests, key_mem, value_mem, peers):
    each = requests.shape[0] // peers
    shape = (peers, each, 2, MB, DH)
    return pl.pallas_call(
        functools.partial(pick_kernel, peers=peers, each=each),
        out_shape=jax.ShapeDtypeStruct(shape, key_mem.dtype),
        in_specs=[
            pl.BlockSpec(memory_space=pltpu.SMEM),
            pl.BlockSpec(memory_space=pl.ANY),
            pl.BlockSpec(memory_space=pl.ANY),
        ],
        out_specs=pl.BlockSpec(memory_space=pl.ANY),
        scratch_shapes=[
            pltpu.VMEM(shape, key_mem.dtype),
            pltpu.SemaphoreType.DMA((peers,)),
            pltpu.SemaphoreType.DMA,
        ],
        compiler_params=pltpu.CompilerParams(vmem_limit_bytes=56 << 20),
        name="pick",
    )(requests, key_mem, value_mem)


def softmax_dot(scores, value):
    top = jnp.max(scores, axis=1, keepdims=True)
    raised = jnp.exp2((scores - top) * SCALE2)
    total = jnp.sum(raised, axis=1, keepdims=True)
    out = jnp.dot(raised.astype(jnp.bfloat16), value, preferred_element_type=jnp.float32)
    return out / total


def scores_of(query, key):
    return lax.dot_general(query, key, (((1,), (1,)), ((), ())), preferred_element_type=jnp.float32)


def band_kernel(*refs):
    own, before = refs[:GROUP], refs[GROUP : 2 * GROUP]
    out_ref, query, key, value = refs[2 * GROUP :]
    rows = query.shape[1]
    behind = BEHIND * rows
    place = lax.axis_index("blk")
    first = jnp.where(place < GROUP, behind, 0)
    for shift in range(GROUP):
        source = (place % GROUP - shift + GROUP) % GROUP
        at = pl.multiple_of(behind + source * rows, rows)
        query[source] = own[shift][0]
        key[pl.ds(at, rows), :] = own[shift][1]
        value[pl.ds(at, rows), :] = own[shift][2]

        @pl.when(source >= GROUP - BEHIND)
        def _():
            earlier = pl.multiple_of((source - (GROUP - BEHIND)) * rows, rows)
            key[pl.ds(earlier, rows), :] = before[shift][0]
            value[pl.ds(earlier, rows), :] = before[shift][1]

    width = behind + QBLK
    for tile in range(GROUP * rows // QBLK):
        base = tile * QBLK
        member, start = divmod(base, rows)
        scores = scores_of(query[member, start : start + QBLK, :], key[base : base + width, :])
        row = lax.broadcasted_iota(jnp.int32, scores.shape, 0)
        col = lax.broadcasted_iota(jnp.int32, scores.shape, 1)
        allowed = (col >= jnp.maximum(row, first - base)) & (col <= row + behind)
        scores = jnp.where(allowed, scores, LOW)
        result = softmax_dot(scores, value[base : base + width, :])
        shift = (member - place % GROUP + GROUP) % GROUP
        out_ref[shift, start : start + QBLK, :] = result.astype(out_ref.dtype)


def band(own, before):
    _, rows, width = own[0].shape
    return pl.pallas_call(
        band_kernel,
        grid=(width // DH,),
        out_shape=jax.ShapeDtypeStruct((GROUP, rows, width), jnp.bfloat16),
        in_specs=[pl.BlockSpec((3, rows, DH), lambda h: (0, 0, h))] * GROUP
        + [pl.BlockSpec((2, rows, DH), lambda h: (0, 0, h))] * GROUP,
        out_specs=pl.BlockSpec((GROUP, rows, DH), lambda h: (0, 0, h)),
        scratch_shapes=[
            pltpu.VMEM((GROUP, rows, DH), jnp.bfloat16),
            pltpu.VMEM(((GROUP + BEHIND) * rows, DH), jnp.bfloat16),
            pltpu.VMEM(((GROUP + BEHIND) * rows, DH), jnp.bfloat16),
        ],
        cost_estimate=pl.CostEstimate(
            flops=2 * 2 * GROUP * rows * 1024 * width,
            bytes_accessed=GROUP * rows * width * 14,
            transcendentals=GROUP * rows * 1024 * width // DH,
        ),
        compiler_params=pltpu.CompilerParams(vmem_limit_bytes=56 << 20),
        name="band",
    )(*own, *before)


def pack_kernel(member_ref, q_ref, k_ref, v_ref, out_ref):
    out_ref[0, 0] = q_ref[...]
    out_ref[0, 1] = k_ref[...]
    out_ref[0, 2] = v_ref[...]


def pack(member, queries, keys, values):
    rows, width = queries.shape
    part = width // GROUP
    spec = pl.BlockSpec((rows, part), lambda s, m: (0, (m[0] + s) % GROUP))
    return pl.pallas_call(
        pack_kernel,
        grid_spec=pltpu.PrefetchScalarGridSpec(
            num_scalar_prefetch=1,
            grid=(GROUP,),
            in_specs=[spec] * 3,
            out_specs=pl.BlockSpec((1, 3, rows, part), lambda s, m: (s, 0, 0, 0)),
        ),
        out_shape=jax.ShapeDtypeStruct((GROUP, 3, rows, part), queries.dtype),
        compiler_params=pltpu.CompilerParams(vmem_limit_bytes=56 << 20),
        name="pack",
    )(member, queries, keys, values)


def share_heads(packed):
    count = lax.axis_size("blk")

    def target(i, shift):
        return i // GROUP * GROUP + (i + shift) % GROUP

    before = []
    for shift in range(GROUP):
        pairs = [
            (i, target(i, shift) + GROUP) for i in range(count - GROUP) if i % GROUP >= GROUP - BEHIND
        ]
        before.append(lax.ppermute(packed[shift, 1:], "blk", pairs))
    own = [packed[0]]
    for shift in range(1, GROUP):
        own.append(lax.ppermute(packed[shift], "blk", [(i, target(i, shift)) for i in range(count)]))
    return own, before


def return_rows(parts):
    count = lax.axis_size("blk")
    back = [parts[0]]
    for shift in range(1, GROUP):
        pairs = [(i, i // GROUP * GROUP + (i + shift) % GROUP) for i in range(count)]
        back.append(lax.ppermute(parts[shift], "blk", pairs))
    return jnp.stack(back)


def memory_kernel(arrival_ref, gate_ref, q_ref, band_ref, *refs):
    blocks, out_ref = refs[:-1], refs[-1]
    share = gate_ref[pl.program_id(0)]
    for tile in range(len(blocks) // RET):
        part = blocks[tile * RET : (tile + 1) * RET]
        base = tile * QBLK
        key = jnp.concatenate([b[0, 0] for b in part], axis=0)
        value = jnp.concatenate([b[0, 1] for b in part], axis=0)
        memory_out = softmax_dot(scores_of(q_ref[base : base + QBLK, :], key), value)
        mixed = share * memory_out + (1.0 - share) * band_ref[0, base : base + QBLK, :].astype(jnp.float32)
        out_ref[base : base + QBLK, :] = mixed.astype(out_ref.dtype)


def memory(arrival, gate_share, queries, band_out, arrived):
    rows, width = queries.shape
    spec = pl.BlockSpec((rows, DH), lambda h, a, g: (0, h))

    each = H // GROUP
    last = arrival.shape[0] - 1
    band_spec = pl.BlockSpec((1, rows, DH), lambda h, a, g: ((a[last] - h // each + GROUP) % GROUP, 0, h % each))

    def block_spec(tile, j):
        return pl.BlockSpec((1, 2, MB, DH), lambda h, a, g: (a[(tile * H + h) * RET + j], 0, 0, 0))

    picked = [block_spec(t, j) for t in range(rows // QBLK) for j in range(RET)]
    return pl.pallas_call(
        memory_kernel,
        grid_spec=pltpu.PrefetchScalarGridSpec(
            num_scalar_prefetch=2,
            grid=(H,),
            in_specs=[spec, band_spec] + picked,
            out_specs=spec,
        ),
        out_shape=jax.ShapeDtypeStruct((rows, width), jnp.bfloat16),
        name="memory",
    )(arrival, gate_share, queries, band_out, *([arrived] * len(picked)))


def plan_requests(target, local_code, peer_count, peer_slots):
    request_count = target.shape[0]
    order = jnp.arange(request_count, dtype=jnp.int32)
    same_target = (target[:, None] == target[None, :]) & (order[None, :] < order[:, None])
    slot_rank = jnp.sum(same_target.astype(jnp.int32), axis=1)
    arrival = target * peer_slots + slot_rank
    places = jnp.arange(peer_count * peer_slots, dtype=jnp.int32)
    hit = places[:, None] == arrival[None, :]
    requests = jnp.sum(jnp.where(hit, local_code[None, :], 0), axis=1)
    return requests.reshape(peer_count, peer_slots), arrival


def local(queries, keys, values, memory_keys, memory_values, owners, slots, gate_logit):
    target = owners.reshape(-1)
    head_flat = jnp.broadcast_to(jnp.arange(H, dtype=jnp.int32)[None, :, None], owners.shape).reshape(-1)
    peer_count = lax.axis_size("grp") * lax.axis_size("blk")
    capacity = max(2, 5 * target.shape[0] // (4 * peer_count))
    requests, arrival = plan_requests(target, slots.reshape(-1) * H + head_flat, peer_count, capacity)
    member = (lax.axis_index("blk") % GROUP).astype(jnp.int32)[None]
    packed = pack(member, queries, keys, values)
    named = lax.all_to_all(requests, ("grp", "blk"), split_axis=0, concat_axis=0, tiled=True)
    named, packed = lax.optimization_barrier((named, packed))
    own, before = share_heads(packed)
    picked = pick(named.reshape(-1), memory_keys, memory_values, peer_count)
    picked, own, before = lax.optimization_barrier((picked, own, before))
    arrived = lax.all_to_all(picked, ("grp", "blk"), split_axis=0, concat_axis=0, tiled=True)
    arrived = arrived.reshape(peer_count * capacity, 2, MB, DH)
    band_out = return_rows(band(own, before))
    arrival = jnp.concatenate([arrival, member])
    return memory(arrival, jax.nn.sigmoid(gate_logit), queries, band_out, arrived)


def solution(mesh):
    rows = P(("grp", "blk"), None)
    blocks = P(("grp", "blk"), None, None)
    return jax.shard_map(
        local,
        mesh=mesh,
        in_specs=(rows, rows, rows, blocks, blocks, blocks, blocks, P()),
        out_specs=rows,
        check_vma=False,
    )
```
